256 devices in a mesh: dp: 4 (over z_hi, core), row: 16 (over x, y), col: 4 (over z_lo).
Axes of the slice: x: 4, y: 4, z: 8 (z_hi: 2, z_lo: 4; z = z_hi * 4 + z_lo), core: 2. Of those that a mesh axis runs over, the one named last changes fastest.
Arguments:
- key_rows: bfloat16 [2048, 4096], P('dp', 'row'), may hold values from -6 to 6
- value_rows: bfloat16 [2048, 4096], P('dp', 'row'), may hold values from -6 to 6
- query_rows: bfloat16 [2048, 4096], P('dp', 'row'), may hold values from -6 to 6
- token_rates: float32 [2048], P('dp'), may hold values from 0.0003 to 0.003
- gate_weight: bfloat16 [4096, 8192], P('row', 'col'), may hold values from -0.09375 to 0.09375
- up_weight: bfloat16 [4096, 8192], P('row', 'col'), may hold values from -0.09375 to 0.09375
- down_weight: bfloat16 [8192, 4096], P('col', 'row'), may hold values from -0.0625 to 0.0625
Outputs:
- applied: bfloat16 [2048, 4096], P(('dp', 'col'), 'row')
The draws below stay inside these ranges and needn't reach their ends.
All inputs are finite; a program needn't handle non-finite values.
Results may differ from the reference program's by a relative error of at most 0.03.
Values may be sent and summed in bfloat16 or wider, within the bound.
No kernel may reach another device: no remote copies, remote signals or barrier semaphores. Data moves between devices by JAX's collectives and lax.ppermute only.
A program may use at most 64 MiB of HBM per device.

```python
import math
import jax
import jax.numpy as jnp

D = 4096
FF = 8192
TOKENS = 2048


def steps_of(stream_key, extent, pieces, smallest, largest):
    level = 1.0
    for axis_at, shards_of in pieces:
        draws = jax.random.uniform(jax.random.fold_in(jax.random.fold_in(stream_key, 6), axis_at), (shards_of,), jnp.float32, smallest / len(pieces), largest / len(pieces))
        level = level * jnp.repeat(jnp.exp(draws), extent[axis_at] // shards_of).reshape((-1,) + (1,) * (len(extent) - 1 - axis_at))
    return level


def scatter_about(own_key, shape, scale, limit, split=(), held_as=jnp.bfloat16):
    drawn = jax.random.normal(own_key, shape, jnp.float32) * scale
    if len(split) > 0:
        drawn = steps_of(own_key, shape, split, -0.22, 0.18) * drawn
    return jnp.clip(drawn, min=-limit, max=limit).astype(held_as)


def setup_inputs(seed: int = 0) -> dict:
    streams_of = jax.random.split(jax.random.key(seed), 8)
    key_rows = scatter_about(streams_of[0], (TOKENS, D), 1.0, 6.0, ((0, 4), (1, 16)))
    value_rows = scatter_about(streams_of[1], (TOKENS, D), 1.0, 6.0, ((0, 4), (1, 16)))
    query_rows = scatter_about(streams_of[2], (TOKENS, D), 1.0, 6.0, ((0, 4), (1, 16)))
    token_rates = jnp.clip(jnp.exp(math.log(0.003) - 2.3025851 * jax.random.uniform(streams_of[3], (TOKENS,), jnp.float32) ** steps_of(streams_of[3], (TOKENS,), ((0, 4),), -0.2, 0.2)), 0.0003, 0.003)
    gate_weight = scatter_about(streams_of[4], (D, FF), D ** -0.5, 0.09375, ((0, 16), (1, 4)))
    up_weight = scatter_about(streams_of[5], (D, FF), D ** -0.5, 0.09375, ((0, 16), (1, 4)))
    down_weight = scatter_about(streams_of[6], (FF, D), FF ** -0.5, 0.0625, ((0, 4), (1, 16)))
    return dict(key_rows=key_rows, value_rows=value_rows, query_rows=query_rows, token_rates=token_rates, gate_weight=gate_weight, up_weight=up_weight, down_weight=down_weight)


def reference(key_rows, value_rows, query_rows, token_rates, gate_weight, up_weight, down_weight):
    scaled = (token_rates[:, None] * value_rows.astype(jnp.float32)).astype(jnp.bfloat16)
    gate_sum = jnp.dot(key_rows, gate_weight, preferred_element_type=jnp.float32)
    up_sum = jnp.dot(key_rows, up_weight, preferred_element_type=jnp.float32)
    back_sum = jnp.dot(scaled, down_weight.T, preferred_element_type=jnp.float32)
    sigmoid_gate = jax.nn.sigmoid(gate_sum)
    activated = gate_sum * sigmoid_gate
    hidden = (activated * up_sum).astype(jnp.bfloat16)
    grad_gate = (back_sum * up_sum * sigmoid_gate * (1.0 + gate_sum * (1.0 - sigmoid_gate))).astype(jnp.bfloat16)
    grad_up = (back_sum * activated).astype(jnp.bfloat16)
    new_gate = (gate_weight.astype(jnp.float32) + jnp.dot(key_rows.T, grad_gate, preferred_element_type=jnp.float32)).astype(jnp.bfloat16)
    new_up = (up_weight.astype(jnp.float32) + jnp.dot(key_rows.T, grad_up, preferred_element_type=jnp.float32)).astype(jnp.bfloat16)
    new_down = (down_weight.astype(jnp.float32) + jnp.dot(hidden.T, scaled, preferred_element_type=jnp.float32)).astype(jnp.bfloat16)
    query_gate = jnp.dot(query_rows, new_gate, preferred_element_type=jnp.float32)
    query_up = jnp.dot(query_rows, new_up, preferred_element_type=jnp.float32)
    query_hidden = (query_gate * jax.nn.sigmoid(query_gate) * query_up).astype(jnp.bfloat16)
    return jnp.dot(query_hidden, new_down, preferred_element_type=jnp.float32).astype(jnp.bfloat16)
```

```python
import jax
import jax.numpy as jnp
from jax import lax
from jax.sharding import Mesh, PartitionSpec as P

SIDE = 4
BF16 = jnp.bfloat16
F32 = jnp.float32


def shifted(value, axis, by):
    return lax.ppermute(value, axis, [(i, (i + by) % SIDE) for i in range(SIDE)])


def swapped(value, axis):
    return lax.ppermute(value, axis, [(0, 1), (1, 0)])


def mm(a, b, ca=1, cb=0):
    return lax.dot_general(a, b, (((ca,), (cb,)), ((), ())), preferred_element_type=F32)


def rolled(value, at):
    size = value.shape[0] // SIDE
    return lax.dynamic_slice_in_dim(jnp.concatenate([value, value]), at * size, value.shape[0], 0)


def collect_y(own):
    return jnp.concatenate([own] + [shifted(own, "y", -k) for k in range(1, SIDE)], axis=1)


def reduce_x(summed):
    size = summed.shape[0] // SIDE
    sent = summed.astype(BF16)
    total = summed[:size]
    for k in range(1, SIDE):
        total = total + shifted(sent[k * size : (k + 1) * size], "x", k).astype(F32)
    return total


def collect_x(own):
    return jnp.concatenate([own] + [shifted(own, "x", -k) for k in range(1, SIDE)], axis=0)


def body(key_rows, value_rows, query_rows, token_rates, gate_weight, up_weight, down_weight):
    zh, core, x, y = (lax.axis_index(a) for a in ("zh", "core", "x", "y"))
    scaled = (token_rates[:, None] * value_rows.astype(F32)).astype(BF16)
    key_scaled = rolled(jnp.concatenate([key_rows, scaled], axis=1), x)
    query = rolled(query_rows, x)
    width = key_rows.shape[1]
    units = gate_weight.shape[1] // 16

    def piece(k):
        at = ((zh * 2 + core) * SIDE + (y + k) % SIDE) * units
        return jnp.concatenate(
            [
                lax.dynamic_slice_in_dim(gate_weight, at, units, 1),
                lax.dynamic_slice_in_dim(up_weight, at, units, 1),
                lax.dynamic_slice_in_dim(down_weight, at, units, 0).T,
            ],
            axis=1,
        )

    with jax.named_scope("weights"):
        own_half = jnp.concatenate(
            [piece(0)] + [shifted(piece(SIDE - k), "y", -k) for k in range(1, SIDE)], axis=0
        )
        other_half = swapped(own_half, "core")
        gate_up = jnp.concatenate([own_half[:, : 2 * units], other_half[:, : 2 * units]], axis=1)
        down = jnp.concatenate([own_half[:, 2 * units :], other_half[:, 2 * units :]], axis=1)

    with jax.named_scope("tokens"):
        keys, scaleds, queries = [], [], []
        for ks in (key_scaled, swapped(key_scaled, "zh")):
            parts = [ks] + [shifted(ks, "y", -k) for k in range(1, SIDE)]
            keys.append(jnp.concatenate([p[:, :width] for p in parts], axis=1))
            scaleds.append(jnp.concatenate([p[:, width:] for p in parts], axis=1))
        for q in (query, swapped(query, "zh")):
            queries.append(collect_y(q))

    delta_gate_up, delta_down = 0.0, 0.0
    with jax.named_scope("inner"):
        for key, scl in zip(keys, scaleds):
            summed = reduce_x(jnp.concatenate([mm(key, gate_up), mm(scl, down)], axis=1))
            pieces = [summed[:, i * units : (i + 1) * units] for i in range(6)]
            gate_sum = jnp.concatenate([pieces[0], pieces[2]], axis=1)
            up_sum = jnp.concatenate([pieces[1], pieces[3]], axis=1)
            back_sum = jnp.concatenate([pieces[4], pieces[5]], axis=1)
            s = jax.nn.sigmoid(gate_sum)
            act = gate_sum * s
            hidden = (act * up_sum).astype(BF16)
            grad_gate = (back_sum * up_sum * s * (1.0 + gate_sum * (1.0 - s))).astype(BF16)
            grad_up = (back_sum * act).astype(BF16)
            grads = collect_x(
                jnp.concatenate(
                    [
                        grad_gate[:, :units],
                        grad_up[:, :units],
                        grad_gate[:, units:],
                        grad_up[:, units:],
                        hidden,
                    ],
                    axis=1,
                )
            )
            delta_gate_up += mm(key, grads[:, : 4 * units], 0, 0)
            delta_down += mm(scl, grads[:, 4 * units :], 0, 0)
    with jax.named_scope("update"):
        theirs = swapped(
            jnp.concatenate([delta_gate_up, delta_down], axis=1).astype(BF16), "core"
        ).astype(F32)
        theirs_gate_up = jnp.concatenate(
            [theirs[:, 2 * units : 4 * units], theirs[:, : 2 * units]], axis=1
        )
        theirs_down = jnp.concatenate([theirs[:, 5 * units :], theirs[:, 4 * units : 5 * units]], axis=1)
        new_gate_up = (gate_up.astype(F32) + (delta_gate_up + theirs_gate_up)).astype(BF16)
        new_down = (down.astype(F32) + (delta_down + theirs_down)).astype(BF16)

    with jax.named_scope("apply"):
        outs = []
        for q in queries:
            summed = reduce_x(mm(q, new_gate_up))
            pieces = [summed[:, i * units : (i + 1) * units] for i in range(4)]
            q_gate = jnp.concatenate([pieces[0], pieces[2]], axis=1)
            q_up = jnp.concatenate([pieces[1], pieces[3]], axis=1)
            q_hidden = collect_x((q_gate * jax.nn.sigmoid(q_gate) * q_up).astype(BF16))
            applied = mm(q_hidden, new_down, 1, 1)
            sent = applied.astype(BF16)
            total = applied[:, :width]
            for k in range(1, SIDE):
                total = total + shifted(sent[:, k * width : (k + 1) * width], "y", k).astype(F32)
            outs.append(rolled(total.astype(BF16), (SIDE - x) % SIDE))
    with jax.named_scope("deliver"):
        low = jnp.where(zh == 0, outs[0], outs[1])
        high = jnp.where(zh == 0, outs[1], outs[0])
        both = jnp.concatenate([low, high]).reshape(2 * SIDE, -1, width)
        came = lax.all_to_all(both, ("zh", "zl"), 0, 0)
        return came.astype(F32).sum(0).astype(BF16)


def solution(mesh):
    fine = Mesh(mesh.devices.reshape(2, 2, SIDE, SIDE, SIDE), ("zh", "core", "x", "y", "zl"))
    dp, row, col = ("zh", "core"), ("x", "y"), "zl"
    placed = (P(dp, row), P(dp, row), P(dp, row), P(dp), P(row, col), P(row, col), P(col, row))
    return jax.shard_map(
        body, mesh=fine, in_specs=placed, out_specs=P(("zh", "core", "zl"), row), check_vma=False
    )
```

```python
import jax
import jax.numpy as jnp
from jax import lax
from jax.experimental import pallas as pl
from jax.sharding import Mesh, PartitionSpec as P

SIDE = 4
BF16 = jnp.bfloat16
F32 = jnp.float32


def shifted(value, axis, by):
    return lax.ppermute(value, axis, [(i, (i + by) % SIDE) for i in range(SIDE)])


def swapped(value, axis):
    return lax.ppermute(value, axis, [(0, 1), (1, 0)])


def mirrored(value):
    last = 2 * SIDE - 1
    return lax.ppermute(value, ("zh", "zl"), [(i, last - i) for i in range(2 * SIDE)])


def after(value, *others):
    anywhere = pl.BlockSpec(memory_space=pl.ANY)
    return pl.pallas_call(
        lambda *refs: None,
        out_shape=jax.ShapeDtypeStruct(value.shape, value.dtype),
        in_specs=[anywhere] * (1 + len(others)),
        out_specs=anywhere,
        input_output_aliases={0: 0},
        name="after",
    )(value, *others)


def mm(a, b, ca=1, cb=0):
    return lax.dot_general(a, b, (((ca,), (cb,)), ((), ())), preferred_element_type=F32)


def rolled(value, at):
    size = value.shape[0] // SIDE
    return lax.dynamic_slice_in_dim(jnp.concatenate([value, value]), at * size, value.shape[0], 0)


def collect_y(own):
    half = own.shape[0] // 2
    before = shifted(own, "y", 1)
    behind = shifted(own, "y", -1)
    far = [shifted(behind[:half], "y", -1), shifted(before[half:], "y", 1)]
    return [own, behind, jnp.concatenate(far, axis=0), before]


def reduce_rows(summed, axis):
    size = summed.shape[0] // SIDE
    sent = summed.astype(BF16)
    total = summed[:size]
    for k in range(1, SIDE):
        total = total + shifted(sent[k * size : (k + 1) * size], axis, k).astype(F32)
    return total


def collect_x(own):
    return jnp.concatenate([own] + [shifted(own, "x", -k) for k in range(1, SIDE)], axis=0)


def body(key_rows, value_rows, query_rows, token_rates, gate_weight, up_weight, down_weight):
    zh, core, x, y = (lax.axis_index(a) for a in ("zh", "core", "x", "y"))
    scaled = (token_rates[:, None] * value_rows.astype(F32)).astype(BF16)
    key_scaled = rolled(jnp.concatenate([key_rows, scaled], axis=1), x)
    query = rolled(query_rows, x)
    width = key_rows.shape[1]
    units = gate_weight.shape[1] // 16

    def piece(k):
        at = ((zh * 2 + core) * SIDE + (y + k) % SIDE) * units
        return jnp.concatenate(
            [
                lax.dynamic_slice_in_dim(gate_weight, at, units, 1),
                lax.dynamic_slice_in_dim(up_weight, at, units, 1),
                lax.dynamic_slice_in_dim(down_weight, at, units, 0).T,
            ],
            axis=1,
        )

    with jax.named_scope("weights"):
        own_half = jnp.concatenate(
            [piece(0)] + [shifted(piece(SIDE - k), "y", -k) for k in range(1, SIDE)], axis=0
        )
        other_half = swapped(own_half, "core")
        gate_up = jnp.concatenate([own_half[:, : 2 * units], other_half[:, : 2 * units]], axis=1)
        down = jnp.concatenate([own_half[:, 2 * units :], other_half[:, 2 * units :]], axis=1)

    with jax.named_scope("tokens"):
        theirs = mirrored(key_scaled)
        gathered = [collect_y(key_scaled), collect_y(theirs)]
        keys = [jnp.concatenate([p[:, :width] for p in parts], axis=1) for parts in gathered]
        scaleds = [jnp.concatenate([p[:, width:] for p in parts], axis=1) for parts in gathered]
    with jax.named_scope("queries"):
        both = jnp.concatenate([mirrored(after(query, theirs)), query], axis=0)
        query_parts = collect_y(after(both, gathered[1][2]))
        half = query.shape[0]
        queries = [
            jnp.concatenate([p[i * half : (i + 1) * half] for p in query_parts], axis=1)
            for i in range(2)
        ]

    delta_gate_up, delta_down = 0.0, 0.0
    with jax.named_scope("inner"):
        for key, scl in zip(keys, scaleds):
            summed = reduce_rows(jnp.concatenate([mm(key, gate_up), mm(scl, down)], axis=1), "x")
            pieces = [summed[:, i * units : (i + 1) * units] for i in range(6)]
            gate_sum = jnp.concatenate([pieces[0], pieces[2]], axis=1)
            up_sum = jnp.concatenate([pieces[1], pieces[3]], axis=1)
            back_sum = jnp.concatenate([pieces[4], pieces[5]], axis=1)
            s = jax.nn.sigmoid(gate_sum)
            act = gate_sum * s
            hidden = (act * up_sum).astype(BF16)
            grad_gate = (back_sum * up_sum * s * (1.0 + gate_sum * (1.0 - s))).astype(BF16)
            grad_up = (back_sum * act).astype(BF16)
            grads = collect_x(
                jnp.concatenate(
                    [
                        grad_gate[:, :units],
                        grad_up[:, :units],
                        grad_gate[:, units:],
                        grad_up[:, units:],
                        hidden,
                    ],
                    axis=1,
                )
            )
            if scl is scaleds[1]:
                grads = after(grads, query_parts[2])
            delta_gate_up += mm(key, grads[:, : 4 * units], 0, 0)
            delta_down += mm(scl, grads[:, 4 * units :], 0, 0)
    with jax.named_scope("update"):
        theirs = swapped(
            jnp.concatenate([delta_gate_up, delta_down], axis=1).astype(BF16), "core"
        ).astype(F32)
        theirs_gate_up = jnp.concatenate(
            [theirs[:, 2 * units : 4 * units], theirs[:, : 2 * units]], axis=1
        )
        theirs_down = jnp.concatenate([theirs[:, 5 * units :], theirs[:, 4 * units : 5 * units]], axis=1)
        new_gate_up = (gate_up.astype(F32) + (delta_gate_up + theirs_gate_up)).astype(BF16)
        new_down = (down.astype(F32) + (delta_down + theirs_down)).astype(BF16)

    with jax.named_scope("apply"):
        outs = []
        for q in queries:
            summed = reduce_rows(mm(q, new_gate_up), "x")
            pieces = [summed[:, i * units : (i + 1) * units] for i in range(4)]
            q_gate = jnp.concatenate([pieces[0], pieces[2]], axis=1)
            q_up = jnp.concatenate([pieces[1], pieces[3]], axis=1)
            q_hidden = collect_x((q_gate * jax.nn.sigmoid(q_gate) * q_up).astype(BF16))
            applied = mm(q_hidden, new_down, 1, 1)
            sent = applied.astype(BF16)
            total = applied[:, :width]
            for k in range(1, SIDE):
                total = total + shifted(sent[:, k * width : (k + 1) * width], "y", k).astype(F32)
            outs.append(total)
    with jax.named_scope("deliver"):
        total = outs[1] + mirrored(outs[0].astype(BF16)).astype(F32)
        total = rolled(total, (lax.axis_index("zl") - x + SIDE) % SIDE)
        return reduce_rows(total, "zl").astype(BF16)


def solution(mesh):
    fine = Mesh(mesh.devices.reshape(2, 2, SIDE, SIDE, SIDE), ("zh", "core", "x", "y", "zl"))
    dp, row, col = ("zh", "core"), ("x", "y"), "zl"
    placed = (P(dp, row), P(dp, row), P(dp, row), P(dp), P(row, col), P(row, col), P(col, row))
    return jax.shard_map(
        body, mesh=fine, in_specs=placed, out_specs=P(("zh", "core", "zl"), row), check_vma=False
    )
```

```python
import jax
import jax.numpy as jnp
from jax import lax
from jax.experimental import pallas as pl
from jax.experimental.pallas import tpu as pltpu
from jax.sharding import Mesh, PartitionSpec as P

SIDE = 4
PART = 128
BF16 = jnp.bfloat16
F32 = jnp.float32
VMEM = pl.BlockSpec(memory_space=pltpu.VMEM)
SMEM = pl.BlockSpec(memory_space=pltpu.SMEM)
ANY = pl.BlockSpec(memory_space=pl.ANY)


def shape(dims, dtype=BF16):
    return jax.ShapeDtypeStruct(dims, dtype)


def call(kernel, name, outs, idx, *operands, waits=(), scratch=(), places=None, flops=0):
    given = (idx, *operands, *waits)
    specs = [SMEM] + (places or [VMEM] * len(operands)) + [ANY] * len(waits)
    n_waits, n_read = len(waits), 1 + len(operands)

    def run(*refs):
        kernel(*refs[:n_read], *refs[n_read + n_waits :])

    moved = sum(o.size * o.dtype.itemsize for o in (*operands, *outs))
    return pl.pallas_call(
        run,
        out_shape=outs,
        in_specs=specs,
        out_specs=[VMEM] * len(outs),
        scratch_shapes=list(scratch),
        compiler_params=pltpu.CompilerParams(vmem_limit_bytes=20 * 2**20),
        cost_estimate=pl.CostEstimate(flops=flops, bytes_accessed=moved, transcendentals=0),
        name=name,
    )(*given)


def after(value, *others):
    return pl.pallas_call(
        lambda *refs: None,
        out_shape=shape(value.shape, value.dtype),
        in_specs=[ANY] * (1 + len(others)),
        out_specs=ANY,
        input_output_aliases={0: 0},
        name="after",
    )(value, *others)


def shifted(value, axis, by):
    return lax.ppermute(value, axis, [(i, (i + by) % SIDE) for i in range(SIDE)])


def swapped(value, axis):
    return lax.ppermute(value, axis, [(0, 1), (1, 0)])


def mirrored(value):
    last = 2 * SIDE - 1
    return lax.ppermute(value, ("zh", "zl"), [(i, last - i) for i in range(2 * SIDE)])


def nt(a, b):
    return lax.dot_general(a, b, (((1,), (1,)), ((), ())), preferred_element_type=F32)


def nn(a, b):
    return jnp.dot(a, b, preferred_element_type=F32)


def block_of(at):
    return pl.ds(pl.multiple_of(lax.rem(at, SIDE) * PART, PART), PART)


def collect_y(own):
    half = own.shape[0] // 2
    before = shifted(own, "y", 1)
    behind = shifted(own, "y", -1)
    far = [shifted(behind[:half], "y", -1), shifted(before[half:], "y", 1)]
    return [own, behind, *far, before]


def collect_x(own):
    return [own] + [shifted(own, "x", -k) for k in range(1, SIDE)]


def scatter(own, sends, axis):
    return [own] + [shifted(s, axis, k + 1) for k, s in enumerate(sends)]


def pieces_kernel(idx, gate, up, down, p0, p1, p2, p3, other0, g, u, d, sems):
    window = pl.ds(pl.multiple_of(idx[0] * 8 * PART, PART), 8 * PART)
    copies = [
        pltpu.make_async_copy(gate.at[:, window], g, sems.at[0]),
        pltpu.make_async_copy(up.at[:, window], u, sems.at[1]),
        pltpu.make_async_copy(down.at[window, :], d, sems.at[2]),
    ]
    for c in copies:
        c.start()
    for c in copies:
        c.wait()
    core, y = idx[1], idx[3]
    for k, out in enumerate((p0, p1, p2, p3, other0)):
        half = core if k < SIDE else 1 - core
        at = pl.multiple_of((half * SIDE + lax.rem(y + k % SIDE, SIDE)) * PART, PART)
        out[:PART] = g[:, pl.ds(at, PART)].T
        out[PART : 2 * PART] = u[:, pl.ds(at, PART)].T
        out[2 * PART :] = d[pl.ds(at, PART), :]


def weights_kernel(idx, w0, w1, w2, w3, o0, others, full):
    rows, width = w0.shape
    for j, w in enumerate((w0, w1, w2, w3)):
        columns = slice(j * width, (j + 1) * width)
        full[:rows, columns] = w[...]
        full[rows:, columns] = o0[...] if j == 0 else others[(j - 1) * rows : j * rows]


def sums_kernel(idx, b0, b1, b2a, b2b, b3, weights, own, s1, s2, s3, total):
    size, width = b0.shape[0] // 2, b0.shape[1] // 2
    for t, far in enumerate((b2a, b2b)):
        rows = slice(t * size, (t + 1) * size)
        key, scl = (
            jnp.concatenate([b0[rows, c], b1[rows, c], far[:, c], b3[rows, c]], axis=1)
            for c in (slice(0, width), slice(width, 2 * width))
        )
        for h in range(2):
            at = h * 3 * PART
            total[rows, at : at + 2 * PART] = nt(key, weights[at : at + 2 * PART])
            total[rows, at + 2 * PART : at + 3 * PART] = nt(scl, weights[at + 2 * PART : at + 3 * PART])
    x = idx[2]
    own[...] = total[block_of(x)]
    for k, s in enumerate((s1, s2, s3)):
        s[...] = total[block_of(x + k + 1)].astype(BF16)


def grads_kernel(idx, own, r1, r2, r3, out):
    for h in range(2):
        at = h * 3 * PART
        gate, up, back = (
            own[:, c] + r1[:, c].astype(F32) + r2[:, c].astype(F32) + r3[:, c].astype(F32)
            for c in (slice(at + i * PART, at + (i + 1) * PART) for i in range(3))
        )
        s = jax.nn.sigmoid(gate)
        act = gate * s
        out[at : at + PART] = (back * up * s * (1.0 + gate * (1.0 - s))).astype(BF16).T
        out[at + PART : at + 2 * PART] = (back * act).astype(BF16).T
        out[at + 2 * PART : at + 3 * PART] = (act * up).astype(BF16).T


def delta_kernel(idx, *refs):
    blocks = [refs[0:5], refs[5:10]]
    grads = [refs[10:14], refs[14:18]]
    out, full = refs[18:]
    x = idx[2]
    tokens = SIDE * PART
    for c in range(2):
        for k in range(SIDE):
            at = pl.multiple_of(c * tokens + lax.rem(x + k, SIDE) * PART, PART)
            full[:, pl.ds(at, PART)] = grads[c][k][...]
    width = blocks[0][0].shape[1] // 2
    for j in range(SIDE):
        parts = []
        for b in blocks:
            parts += [b[2], b[3]] if j == 2 else [b[j if j < 2 else 4]]
        columns = slice(j * width, (j + 1) * width)
        key = jnp.concatenate([p[:, :width] for p in parts], axis=0)
        for h in range(2):
            at = h * 3 * PART
            out[at : at + 2 * PART, columns] = nn(full[at : at + 2 * PART], key).astype(BF16)
        scl = jnp.concatenate([p[:, width:] for p in parts], axis=0)
        for h in range(2):
            rows = slice(h * 3 * PART + 2 * PART, (h + 1) * 3 * PART)
            out[rows, columns] = nn(full[rows], scl).astype(BF16)


def query_kernel(idx, weights, mine, theirs, q0, q1, q2a, q2b, q3, *refs):
    outs, new_down, fresh, total = (refs[0:4], refs[4:8]), refs[8], refs[9], refs[10]
    half = 3 * PART
    for h in range(2):
        rows, swap = slice(h * half, (h + 1) * half), slice((1 - h) * half, (2 - h) * half)
        added = mine[rows].astype(F32) + theirs[swap].astype(F32)
        fresh[rows] = (weights[rows].astype(F32) + added).astype(BF16)
        new_down[h * PART : (h + 1) * PART] = fresh[h * half + 2 * PART : (h + 1) * half]
    x = idx[2]
    tokens = SIDE * PART
    for c, far in enumerate((q2a, q2b)):
        rows = slice(c * tokens, (c + 1) * tokens)
        query = jnp.concatenate([q0[rows], q1[rows], far[...], q3[rows]], axis=1)
        for h in range(2):
            total[:, h * 2 * PART : (h + 1) * 2 * PART] = nt(query, fresh[h * half : h * half + 2 * PART])
        outs[c][0][...] = total[block_of(x)]
        for k in range(1, SIDE):
            outs[c][k][...] = total[block_of(x + k)].astype(BF16)


def silu_kernel(idx, own, r1, r2, r3, out):
    for h in range(2):
        at = h * 2 * PART
        gate, up = (
            own[:, c] + r1[:, c].astype(F32) + r2[:, c].astype(F32) + r3[:, c].astype(F32)
            for c in (slice(at, at + PART), slice(at + PART, at + 2 * PART))
        )
        out[:, h * PART : (h + 1) * PART] = (gate * jax.nn.sigmoid(gate) * up).astype(BF16)


def apply_kernel(idx, h0, h1, h2, h3, new_down, own, s1, s2, s3, full):
    x = idx[2]
    for k, h in enumerate((h0, h1, h2, h3)):
        full[block_of(x + k)] = h[...]
    width = own.shape[1]
    for k, out in enumerate((own, s1, s2, s3)):
        out[...] = nn(full[...], new_down[:, k * width : (k + 1) * width]).astype(out.dtype)


def add_kernel(idx, own, r1, r2, r3, out):
    total = own[...] + r1[...].astype(F32) + r2[...].astype(F32) + r3[...].astype(F32)
    out[...] = total.astype(out.dtype)


def join_kernel(idx, own, r1, r2, r3, came, mine, s1, s2, s3, total):
    total[...] = (
        own[...] + r1[...].astype(F32) + r2[...].astype(F32) + r3[...].astype(F32) + came[...].astype(F32)
    )
    zl = idx[4]
    for k, out in enumerate((mine, s1, s2, s3)):
        out[...] = total[block_of(zl + k)].astype(out.dtype)


def body(key_rows, value_rows, query_rows, token_rates, gate_weight, up_weight, down_weight):
    idx = jnp.stack([lax.axis_index(a) for a in ("zh", "core", "x", "y", "zl")]).astype(jnp.int32)
    scaled = (token_rates[:, None] * value_rows.astype(F32)).astype(BF16)
    tokens, width = key_rows.shape
    model = SIDE * width
    half = 3 * PART
    key_scaled = jnp.concatenate([key_rows, scaled], axis=1)

    piece = shape((half, width))
    p = call(
        pieces_kernel, "pieces", [piece] * 5, idx, gate_weight, up_weight, down_weight,
        places=[ANY] * 3,
        scratch=[
            pltpu.VMEM((width, 8 * PART), BF16),
            pltpu.VMEM((width, 8 * PART), BF16),
            pltpu.VMEM((8 * PART, width), BF16),
            pltpu.SemaphoreType.DMA((3,)),
        ],
    )
    w = [shifted(p[SIDE - k], "y", -k) for k in range(1, SIDE)]
    others = swapped(jnp.concatenate(w, axis=0), "core")
    weights = call(weights_kernel, "weights", [shape((2 * half, model))], idx, p[0], *w, p[4], others)[0]

    theirs = mirrored(key_scaled)
    sent_sum = shape((PART, 2 * half))
    blocks, grads = [], []
    for chunk in (key_scaled, theirs):
        blocks.append(collect_y(chunk))
        own, *sends = call(
            sums_kernel, "sums", [shape((PART, 2 * half), F32)] + [sent_sum] * 3, idx, *blocks[-1], weights,
            scratch=[pltpu.VMEM((tokens, 2 * half), F32)], flops=2 * tokens * model * 2 * half,
        )
        if chunk is theirs:
            both = jnp.concatenate([mirrored(after(query_rows, theirs)), query_rows], axis=0)
            queries = collect_y(after(both, sends[0]))
        parts = scatter(own, sends, "x")
        out = call(grads_kernel, "grads", [shape((2 * half, PART))], idx, *parts)[0]
        grads.append(collect_x(out))

    mine = call(
        delta_kernel, "delta", [shape((2 * half, model))], idx, *blocks[0], *blocks[1], *grads[0], *grads[1],
        waits=queries[2:4],
        scratch=[pltpu.VMEM((2 * half, 2 * tokens), BF16)], flops=2 * 2 * tokens * model * 2 * half,
    )[0]
    partner = swapped(mine, "core")
    sent_query = shape((PART, SIDE * PART))
    *asked, new_down = call(
        query_kernel, "query", ([shape((PART, SIDE * PART), F32)] + [sent_query] * 3) * 2 + [shape((2 * PART, model))],
        idx, weights, mine, partner, *queries,
        scratch=[pltpu.VMEM((2 * half, model), BF16), pltpu.VMEM((tokens, SIDE * PART), F32)],
        flops=2 * 2 * tokens * model * SIDE * PART,
    )
    applied = []
    for c in range(2):
        own, *sends = asked[c * SIDE : (c + 1) * SIDE]
        hidden = call(silu_kernel, "silu", [shape((PART, 2 * PART))], idx, *scatter(own, sends, "x"))[0]
        own, *sends = call(
            apply_kernel, "apply", [shape((tokens, width), F32)] + [shape((tokens, width))] * 3,
            idx, *collect_x(hidden), new_down,
            scratch=[pltpu.VMEM((tokens, 2 * PART), BF16)], flops=2 * tokens * model * 2 * PART,
        )
        applied.append(scatter(own, sends, "y"))
    away = call(add_kernel, "away", [shape((tokens, width))], idx, *applied[0])[0]
    came = mirrored(away)
    own, *sends = call(
        join_kernel, "join", [shape((PART, width), F32)] + [shape((PART, width))] * 3, idx, *applied[1], came,
        scratch=[pltpu.VMEM((tokens, width), F32)],
    )
    return call(add_kernel, "last", [shape((PART, width))], idx, *scatter(own, sends, "zl"))[0]


def solution(mesh):
    fine = Mesh(mesh.devices.reshape(2, 2, SIDE, SIDE, SIDE), ("zh", "core", "x", "y", "zl"))
    dp, row, col = ("zh", "core"), ("x", "y"), "zl"
    placed = (P(dp, row), P(dp, row), P(dp, row), P(dp), P(row, col), P(row, col), P(col, row))
    return jax.shard_map(
        body, mesh=fine, in_specs=placed, out_specs=P(("zh", "core", "zl"), row), check_vma=False
    )
```

```python
import functools

import jax
import jax.numpy as jnp
from jax import lax
from jax.experimental import pallas as pl
from jax.experimental.pallas import tpu as pltpu
from jax.sharding import Mesh, PartitionSpec as P

SIDE = 4
PART = 128
BF16 = jnp.bfloat16
F32 = jnp.float32
VMEM = pl.BlockSpec(memory_space=pltpu.VMEM)
SMEM = pl.BlockSpec(memory_space=pltpu.SMEM)
ANY = pl.BlockSpec(memory_space=pl.ANY)
HBM = pl.BlockSpec(memory_space=pltpu.HBM)


def shape(dims, dtype=BF16):
    return jax.ShapeDtypeStruct(dims, dtype)


def call(kernel, name, outs, idx, *operands, waits=(), scratch=(), places=None, flops=0, limit=8):
    given = (idx, *operands, *waits)
    specs = [SMEM] + (places or [VMEM] * len(operands)) + [ANY] * len(waits)
    n_waits, n_read = len(waits), 1 + len(operands)

    def run(*refs):
        kernel(*refs[:n_read], *refs[n_read + n_waits :])

    moved = sum(o.size * o.dtype.itemsize for o in (*operands, *outs))
    return pl.pallas_call(
        run,
        out_shape=outs,
        in_specs=specs,
        out_specs=[VMEM] * len(outs),
        scratch_shapes=list(scratch),
        compiler_params=pltpu.CompilerParams(vmem_limit_bytes=limit * 2**20),
        cost_estimate=pl.CostEstimate(flops=flops, bytes_accessed=moved, transcendentals=0),
        name=name,
    )(*given)


def after(value, *others):
    return pl.pallas_call(
        lambda *refs: None,
        out_shape=shape(value.shape, value.dtype),
        in_specs=[ANY] * (1 + len(others)),
        out_specs=ANY,
        input_output_aliases={0: 0},
        compiler_params=pltpu.CompilerParams(vmem_limit_bytes=2**20),
        name="after",
    )(value, *others)


def shifted(value, axis, by):
    return lax.ppermute(value, axis, [(i, (i + by) % SIDE) for i in range(SIDE)])


def swapped(value, axis):
    return lax.ppermute(value, axis, [(0, 1), (1, 0)])


def mirrored(value):
    last = 2 * SIDE - 1
    return lax.ppermute(value, ("zh", "zl"), [(i, last - i) for i in range(2 * SIDE)])


def nt(a, b):
    return lax.dot_general(a, b, (((1,), (1,)), ((), ())), preferred_element_type=F32)


def nn(a, b):
    return jnp.dot(a, b, preferred_element_type=F32)


def block_of(at):
    return pl.ds(pl.multiple_of(lax.rem(at, SIDE) * PART, PART), PART)


def near_y(own):
    return shifted(own, "y", -1), shifted(own, "y", 1)


def far_y(idx, behind, before, *waits):
    rows, columns = before.shape
    half = shape((rows // 2, columns))
    halves = call(halves_kernel, "halves", [half, half], idx, behind, before, waits=waits, limit=1)
    return shifted(halves[0], "y", -1), shifted(halves[1], "y", 1)


def collect_x(own):
    return [own] + [shifted(own, "x", -k) for k in range(1, SIDE)]


def scatter(own, sends, axis):
    return [own] + [shifted(s, axis, k + 1) for k, s in enumerate(sends)]


def pack_kernel(idx, key, value, rates, out):
    tokens, width = key.shape
    out[:, :width] = key[...]
    for i in range(tokens // PART):
        rows = slice(i * PART, (i + 1) * PART)
        rate = jnp.broadcast_to(rates[i : i + 1], (PART, PART)).T
        for at in range(0, width, PART):
            scaled = rate * value[rows, at : at + PART].astype(F32)
            out[rows, width + at : width + at + PART] = scaled.astype(BF16)


def halves_kernel(idx, behind, before, first, second):
    half = first.shape[0]
    first[...] = behind[:half]
    second[...] = before[half:]


def stack_kernel(idx, *refs):
    *parts, out = refs
    rows = parts[0].shape[0]
    for i, part in enumerate(parts):
        out[i * rows : (i + 1) * rows] = part[...]


def pieces_kernel(idx, gate, up, down, p0, p1, p2, p3, other0, g, u, d, sems):
    window = pl.ds(pl.multiple_of(idx[0] * 8 * PART, PART), 8 * PART)
    copies = [
        pltpu.make_async_copy(gate.at[:, window], g, sems.at[0]),
        pltpu.make_async_copy(up.at[:, window], u, sems.at[1]),
        pltpu.make_async_copy(down.at[window, :], d, sems.at[2]),
    ]
    for c in copies:
        c.start()
    for c in copies:
        c.wait()
    core, y = idx[1], idx[3]
    for k, out in enumerate((p0, p1, p2, p3, other0)):
        half = core if k < SIDE else 1 - core
        at = pl.multiple_of((half * SIDE + lax.rem(y + k % SIDE, SIDE)) * PART, PART)
        out[:PART] = g[:, pl.ds(at, PART)].T
        out[PART : 2 * PART] = u[:, pl.ds(at, PART)].T
        out[2 * PART :] = d[pl.ds(at, PART), :]


def weights_kernel(idx, w0, w1, w2, w3, o0, others, full):
    rows, width = w0.shape
    for j, w in enumerate((w0, w1, w2, w3)):
        columns = slice(j * width, (j + 1) * width)
        full[:rows, columns] = w[...]
        full[rows:, columns] = o0[...] if j == 0 else others[(j - 1) * rows : j * rows]


def sums_kernel(idx, b0, b1, b2a, b2b, b3, weights, own, s1, s2, s3, total):
    size, width = b0.shape[0] // 2, b0.shape[1] // 2
    for t, far in enumerate((b2a, b2b)):
        rows = slice(t * size, (t + 1) * size)
        key, scl = (
            jnp.concatenate([b0[rows, c], b1[rows, c], far[:, c], b3[rows, c]], axis=1)
            for c in (slice(0, width), slice(width, 2 * width))
        )
        for h in range(2):
            at = h * 3 * PART
            total[rows, at : at + 2 * PART] = nt(key, weights[at : at + 2 * PART])
            total[rows, at + 2 * PART : at + 3 * PART] = nt(scl, weights[at + 2 * PART : at + 3 * PART])
    x = idx[2]
    own[...] = total[block_of(x)]
    for k, s in enumerate((s1, s2, s3)):
        s[...] = total[block_of(x + k + 1)].astype(BF16)


def grads_kernel(idx, own, r1, r2, r3, out):
    for h in range(2):
        at = h * 3 * PART
        gate, up, back = (
            own[:, c] + r1[:, c].astype(F32) + r2[:, c].astype(F32) + r3[:, c].astype(F32)
            for c in (slice(at + i * PART, at + (i + 1) * PART) for i in range(3))
        )
        s = jax.nn.sigmoid(gate)
        act = gate * s
        out[at : at + PART] = (back * up * s * (1.0 + gate * (1.0 - s))).astype(BF16).T
        out[at + PART : at + 2 * PART] = (back * act).astype(BF16).T
        out[at + 2 * PART : at + 3 * PART] = (act * up).astype(BF16).T


def delta_kernel(idx, *refs):
    blocks = [refs[0:5], refs[5:10]]
    grads = [refs[10:14], refs[14:18]]
    out, full = refs[18:]
    x = idx[2]
    tokens = SIDE * PART
    for c in range(2):
        for k in range(SIDE):
            at = pl.multiple_of(c * tokens + lax.rem(x + k, SIDE) * PART, PART)
            full[:, pl.ds(at, PART)] = grads[c][k][...]
    width = blocks[0][0].shape[1] // 2
    for j in range(SIDE):
        parts = []
        for b in blocks:
            parts += [b[2], b[3]] if j == 2 else [b[j if j < 2 else 4]]
        columns = slice(j * width, (j + 1) * width)
        key = jnp.concatenate([p[:, :width] for p in parts], axis=0)
        for h in range(2):
            at = h * 3 * PART
            out[at : at + 2 * PART, columns] = nn(full[at : at + 2 * PART], key).astype(BF16)
        scl = jnp.concatenate([p[:, width:] for p in parts], axis=0)
        for h in range(2):
            rows = slice(h * 3 * PART + 2 * PART, (h + 1) * 3 * PART)
            out[rows, columns] = nn(full[rows], scl).astype(BF16)


def query_kernel(idx, weights, mine, theirs, q0, q1, q2a, q2b, q3, *refs):
    outs, (new_down, fresh, total) = refs[:SIDE], refs[SIDE:]
    half = 3 * PART
    for h in range(2):
        rows, swap = slice(h * half, (h + 1) * half), slice((1 - h) * half, (2 - h) * half)
        added = mine[rows].astype(F32) + theirs[swap].astype(F32)
        fresh[rows] = (weights[rows].astype(F32) + added).astype(BF16)
        new_down[h * PART : (h + 1) * PART] = fresh[h * half + 2 * PART : (h + 1) * half]
    x = idx[2]
    tokens = SIDE * PART
    for c, far in enumerate((q2a, q2b)):
        rows = slice(c * tokens, (c + 1) * tokens)
        query = jnp.concatenate([q0[rows], q1[rows], far[...], q3[rows]], axis=1)
        for h in range(2):
            total[:, h * 2 * PART : (h + 1) * 2 * PART] = nt(query, fresh[h * half : h * half + 2 * PART])
        for k, out in enumerate(outs):
            out[c * PART : (c + 1) * PART] = total[block_of(x + k)].astype(out.dtype)


def silu_kernel(idx, own, r1, r2, r3, out):
    for h in range(2):
        at = h * 2 * PART
        gate, up = (
            own[:, c] + r1[:, c].astype(F32) + r2[:, c].astype(F32) + r3[:, c].astype(F32)
            for c in (slice(at, at + PART), slice(at + PART, at + 2 * PART))
        )
        out[:, h * PART : (h + 1) * PART] = (gate * jax.nn.sigmoid(gate) * up).astype(BF16)


def apply_kernel(chunk, idx, h0, h1, h2, h3, new_down, own, s1, s2, s3, full):
    x = idx[2]
    for k, h in enumerate((h0, h1, h2, h3)):
        full[block_of(x + k)] = h[chunk * PART : (chunk + 1) * PART]
    width = own.shape[1]
    for k, out in enumerate((own, s1, s2, s3)):
        out[...] = nn(full[...], new_down[:, k * width : (k + 1) * width]).astype(out.dtype)


def add_kernel(idx, own, r1, r2, r3, out):
    total = own[...] + r1[...].astype(F32) + r2[...].astype(F32) + r3[...].astype(F32)
    out[...] = total.astype(out.dtype)


def join_kernel(idx, own, r1, r2, r3, came, mine, s1, s2, s3, total):
    total[...] = (
        own[...] + r1[...].astype(F32) + r2[...].astype(F32) + r3[...].astype(F32) + came[...].astype(F32)
    )
    zl = idx[4]
    for k, out in enumerate((mine, s1, s2, s3)):
        out[...] = total[block_of(zl + k)].astype(out.dtype)


def body(key_rows, value_rows, query_rows, token_rates, gate_weight, up_weight, down_weight):
    idx = jnp.stack([lax.axis_index(a) for a in ("zh", "core", "x", "y", "zl")]).astype(jnp.int32)
    tokens, width = key_rows.shape
    model = SIDE * width
    half = 3 * PART
    key_scaled = call(
        pack_kernel, "pack", [shape((tokens, 2 * width))], idx, key_rows, value_rows,
        token_rates.reshape(-1, PART), limit=2,
    )[0]

    piece = shape((half, width))
    p = call(
        pieces_kernel, "pieces", [piece] * 5, idx, gate_weight, up_weight, down_weight,
        places=[HBM] * 3, waits=(key_scaled,), limit=4,
        scratch=[
            pltpu.VMEM((width, 8 * PART), BF16),
            pltpu.VMEM((width, 8 * PART), BF16),
            pltpu.VMEM((8 * PART, width), BF16),
            pltpu.SemaphoreType.DMA((3,)),
        ],
    )
    w = [shifted(p[SIDE - k], "y", -k) for k in range(1, SIDE)]
    stacked = call(stack_kernel, "stack", [shape((3 * half, width))], idx, *w, limit=1)[0]
    others = swapped(stacked, "core")
    weights = call(weights_kernel, "weights", [shape((2 * half, model))], idx, p[0], *w, p[4], others)[0]

    theirs = mirrored(key_scaled)
    sent_sum = shape((PART, 2 * half))
    blocks, grads = [], []
    behind, before = near_y(key_scaled)
    theirs = after(theirs, behind, before)
    near_theirs = near_y(theirs)

    def inner(parts, *waits):
        blocks.append(parts)
        own, *sends = call(
            sums_kernel, "sums", [shape((PART, 2 * half), F32)] + [sent_sum] * 3, idx, *parts, weights,
            waits=waits,
            scratch=[pltpu.VMEM((tokens, 2 * half), F32)], flops=2 * tokens * model * 2 * half,
        )
        pieces = scatter(own, sends, "x")
        out = call(grads_kernel, "grads", [shape((2 * half, PART))], idx, *pieces, limit=4)[0]
        grads.append(collect_x(out))
        return pieces

    summed = inner([key_scaled, behind, *far_y(idx, behind, before), before])
    query_theirs = mirrored(after(query_rows, summed[0]))
    behind, before = near_theirs
    far = far_y(idx, behind, before, summed[0])
    arrived = inner([theirs, behind, *far, before], *grads[0][1:], query_theirs)
    both = call(
        stack_kernel, "queries", [shape((2 * tokens, width))], idx, query_theirs, query_rows,
        waits=arrived[1:], limit=1,
    )[0]
    behind, before = near_y(both)
    queries = [both, behind, *far_y(idx, behind, before), before]

    mine = call(
        delta_kernel, "delta", [shape((2 * half, model))], idx, *blocks[0], *blocks[1], *grads[0], *grads[1],
        waits=(behind, before),
        scratch=[pltpu.VMEM((2 * half, 2 * tokens), BF16)], flops=2 * 2 * tokens * model * 2 * half,
    )[0]
    partner = swapped(mine, "core")
    sent_query = shape((2 * PART, SIDE * PART))
    own, *sends, new_down = call(
        query_kernel, "query", [shape((2 * PART, SIDE * PART), F32)] + [sent_query] * 3 + [shape((2 * PART, model))],
        idx, weights, mine, partner, *queries,
        scratch=[pltpu.VMEM((2 * half, model), BF16), pltpu.VMEM((tokens, SIDE * PART), F32)],
        flops=2 * 2 * tokens * model * SIDE * PART,
    )
    hidden = call(silu_kernel, "silu", [shape((2 * PART, 2 * PART))], idx, *scatter(own, sends, "x"), limit=4)[0]
    hidden = collect_x(hidden)
    applied, done = [], ()
    for c in range(2):
        own, *sends = call(
            functools.partial(apply_kernel, c), "apply", [shape((tokens, width), F32)] + [shape((tokens, width))] * 3,
            idx, *hidden, new_down, waits=done,
            scratch=[pltpu.VMEM((tokens, 2 * PART), BF16)], flops=2 * tokens * model * 2 * PART,
        )
        applied.append(scatter(own, sends, "y"))
        done = (own,)
    away = call(add_kernel, "away", [shape((tokens, width))], idx, *applied[0], limit=4)[0]
    came = mirrored(away)
    own, *sends = call(
        join_kernel, "join", [shape((PART, width), F32)] + [shape((PART, width))] * 3, idx, *applied[1], came,
        scratch=[pltpu.VMEM((tokens, width), F32)],
    )
    return call(add_kernel, "last", [shape((PART, width))], idx, *scatter(own, sends, "zl"))[0]


def solution(mesh):
    fine = Mesh(mesh.devices.reshape(2, 2, SIDE, SIDE, SIDE), ("zh", "core", "x", "y", "zl"))
    dp, row, col = ("zh", "core"), ("x", "y"), "zl"
    placed = (P(dp, row), P(dp, row), P(dp, row), P(dp), P(row, col), P(row, col), P(col, row))
    return jax.shard_map(
        body, mesh=fine, in_specs=placed, out_specs=P(("zh", "core", "zl"), row), check_vma=False
    )
```

```python
import jax
import jax.numpy as jnp
from jax import lax
from jax.experimental import pallas as pl
from jax.experimental.pallas import tpu as pltpu
from jax.sharding import Mesh, PartitionSpec as P

SIDE = 4
PART = 128
BF16 = jnp.bfloat16
F32 = jnp.float32
VMEM = pl.BlockSpec(memory_space=pltpu.VMEM)
SMEM = pl.BlockSpec(memory_space=pltpu.SMEM)
ANY = pl.BlockSpec(memory_space=pl.ANY)
HBM = pl.BlockSpec(memory_space=pltpu.HBM)


def shape(dims, dtype=BF16):
    return jax.ShapeDtypeStruct(dims, dtype)


def call(kernel, name, outs, idx, *operands, waits=(), scratch=(), places=None, flops=0, limit=8):
    given = (idx, *operands, *waits)
    specs = [SMEM] + (places or [VMEM] * len(operands)) + [ANY] * len(waits)
    n_waits, n_read = len(waits), 1 + len(operands)

    def run(*refs):
        kernel(*refs[:n_read], *refs[n_read + n_waits :])

    moved = sum(o.size * o.dtype.itemsize for o in (*operands, *outs))
    return pl.pallas_call(
        run,
        out_shape=outs,
        in_specs=specs,
        out_specs=[VMEM] * len(outs),
        scratch_shapes=list(scratch),
        compiler_params=pltpu.CompilerParams(vmem_limit_bytes=limit * 2**20),
        cost_estimate=pl.CostEstimate(flops=flops, bytes_accessed=moved, transcendentals=0),
        name=name,
    )(*given)


def after(value, *others):
    return pl.pallas_call(
        lambda *refs: None,
        out_shape=shape(value.shape, value.dtype),
        in_specs=[ANY] * (1 + len(others)),
        out_specs=ANY,
        input_output_aliases={0: 0},
        compiler_params=pltpu.CompilerParams(vmem_limit_bytes=2**20),
        name="after",
    )(value, *others)


def shifted(value, axis, by):
    return lax.ppermute(value, axis, [(i, (i + by) % SIDE) for i in range(SIDE)])


def swapped(value, axis):
    return lax.ppermute(value, axis, [(0, 1), (1, 0)])


def mirrored(value):
    last = 2 * SIDE - 1
    return lax.ppermute(value, ("zh", "zl"), [(i, last - i) for i in range(2 * SIDE)])


def nt(a, b):
    return lax.dot_general(a, b, (((1,), (1,)), ((), ())), preferred_element_type=F32)


def nn(a, b):
    return jnp.dot(a, b, preferred_element_type=F32)


def block_of(at):
    return pl.ds(pl.multiple_of(lax.rem(at, SIDE) * PART, PART), PART)


def near_y(own):
    return shifted(own, "y", -1), shifted(own, "y", 1)


def far_y(idx, behind, before, *waits):
    rows, columns = before.shape
    half = shape((rows // 2, columns))
    halves = call(halves_kernel, "halves", [half, half], idx, behind, before, waits=waits, limit=1)
    return shifted(halves[0], "y", -1), shifted(halves[1], "y", 1)


def collect_x(own):
    return [own] + [shifted(own, "x", -k) for k in range(1, SIDE)]


def scatter(own, sends, axis):
    return [own] + [shifted(s, axis, k + 1) for k, s in enumerate(sends)]


def pack_kernel(idx, key, value, rates, out):
    tokens, width = key.shape
    out[:, :width] = key[...]
    for i in range(tokens // PART):
        rows = slice(i * PART, (i + 1) * PART)
        rate = jnp.broadcast_to(rates[i : i + 1], (PART, PART)).T
        for at in range(0, width, PART):
            scaled = rate * value[rows, at : at + PART].astype(F32)
            out[rows, width + at : width + at + PART] = scaled.astype(BF16)


def halves_kernel(idx, behind, before, first, second):
    half = first.shape[0]
    first[...] = behind[:half]
    second[...] = before[half:]


def stack_kernel(idx, *refs):
    *parts, out = refs
    rows = parts[0].shape[0]
    for i, part in enumerate(parts):
        out[i * rows : (i + 1) * rows] = part[...]


def pieces_kernel(idx, gate, up, down, p0, p1, p2, p3, other0, g, u, d, sems):
    window = pl.ds(pl.multiple_of(idx[0] * 8 * PART, PART), 8 * PART)
    copies = [
        pltpu.make_async_copy(gate.at[:, window], g, sems.at[0]),
        pltpu.make_async_copy(up.at[:, window], u, sems.at[1]),
        pltpu.make_async_copy(down.at[window, :], d, sems.at[2]),
    ]
    for c in copies:
        c.start()
    for c in copies:
        c.wait()
    core, y = idx[1], idx[3]
    for k, out in enumerate((p0, p1, p2, p3, other0)):
        half = core if k < SIDE else 1 - core
        at = pl.multiple_of((half * SIDE + lax.rem(y + k % SIDE, SIDE)) * PART, PART)
        out[:PART] = g[:, pl.ds(at, PART)].T
        out[PART : 2 * PART] = u[:, pl.ds(at, PART)].T
        out[2 * PART :] = d[pl.ds(at, PART), :]


def weights_kernel(idx, w0, w1, w2, w3, o0, others, full):
    rows, width = w0.shape
    for j, w in enumerate((w0, w1, w2, w3)):
        columns = slice(j * width, (j + 1) * width)
        full[:rows, columns] = w[...]
        full[rows:, columns] = o0[...] if j == 0 else others[(j - 1) * rows : j * rows]


def sums_kernel(idx, b0, b1, b2a, b2b, b3, weights, own, s1, s2, s3, total):
    size, width = b0.shape[0] // 2, b0.shape[1] // 2
    for t, far in enumerate((b2a, b2b)):
        rows = slice(t * size, (t + 1) * size)
        key, scl = (
            jnp.concatenate([b0[rows, c], b1[rows, c], far[:, c], b3[rows, c]], axis=1)
            for c in (slice(0, width), slice(width, 2 * width))
        )
        for h in range(2):
            at = h * 3 * PART
            total[rows, at : at + 2 * PART] = nt(key, weights[at : at + 2 * PART])
            total[rows, at + 2 * PART : at + 3 * PART] = nt(scl, weights[at + 2 * PART : at + 3 * PART])
    x = idx[2]
    own[...] = total[block_of(x)]
    for k, s in enumerate((s1, s2, s3)):
        s[...] = total[block_of(x + k + 1)].astype(BF16)


def grads_kernel(idx, own, r1, r2, r3, out):
    for h in range(2):
        at = h * 3 * PART
        gate, up, back = (
            own[:, c] + r1[:, c].astype(F32) + r2[:, c].astype(F32) + r3[:, c].astype(F32)
            for c in (slice(at + i * PART, at + (i + 1) * PART) for i in range(3))
        )
        s = jax.nn.sigmoid(gate)
        act = gate * s
        out[at : at + PART] = (back * up * s * (1.0 + gate * (1.0 - s))).astype(BF16).T
        out[at + PART : at + 2 * PART] = (back * act).astype(BF16).T
        out[at + 2 * PART : at + 3 * PART] = (act * up).astype(BF16).T


def delta_kernel(idx, *refs):
    blocks = [refs[0:5], refs[5:10]]
    grads = [refs[10:14], refs[14:18]]
    out, full = refs[18:]
    x = idx[2]
    tokens = SIDE * PART
    for c in range(2):
        for k in range(SIDE):
            at = pl.multiple_of(c * tokens + lax.rem(x + k, SIDE) * PART, PART)
            full[:, pl.ds(at, PART)] = grads[c][k][...]
    width = blocks[0][0].shape[1] // 2
    for j in range(SIDE):
        parts = []
        for b in blocks:
            parts += [b[2], b[3]] if j == 2 else [b[j if j < 2 else 4]]
        columns = slice(j * width, (j + 1) * width)
        key = jnp.concatenate([p[:, :width] for p in parts], axis=0)
        for h in range(2):
            at = h * 3 * PART
            out[at : at + 2 * PART, columns] = nn(full[at : at + 2 * PART], key).astype(BF16)
        scl = jnp.concatenate([p[:, width:] for p in parts], axis=0)
        for h in range(2):
            rows = slice(h * 3 * PART + 2 * PART, (h + 1) * 3 * PART)
            out[rows, columns] = nn(full[rows], scl).astype(BF16)


def query_kernel(idx, weights, mine, theirs, q0, q1, q2a, q2b, q3, *refs):
    outs, (new_down, fresh, total) = (refs[:SIDE], refs[SIDE : 2 * SIDE]), refs[2 * SIDE :]
    half = 3 * PART
    for h in range(2):
        rows, swap = slice(h * half, (h + 1) * half), slice((1 - h) * half, (2 - h) * half)
        added = mine[rows].astype(F32) + theirs[swap].astype(F32)
        fresh[rows] = (weights[rows].astype(F32) + added).astype(BF16)
        new_down[h * PART : (h + 1) * PART] = fresh[h * half + 2 * PART : (h + 1) * half]
    x = idx[2]
    tokens = SIDE * PART
    for c, far in enumerate((q2a, q2b)):
        rows = slice(c * tokens, (c + 1) * tokens)
        query = jnp.concatenate([q0[rows], q1[rows], far[...], q3[rows]], axis=1)
        for h in range(2):
            total[:, h * 2 * PART : (h + 1) * 2 * PART] = nt(query, fresh[h * half : h * half + 2 * PART])
        for k, out in enumerate(outs[c]):
            out[...] = total[block_of(x + k)].astype(out.dtype)


def silu_kernel(idx, own, r1, r2, r3, out):
    for h in range(2):
        at = h * 2 * PART
        gate, up = (
            own[:, c] + r1[:, c].astype(F32) + r2[:, c].astype(F32) + r3[:, c].astype(F32)
            for c in (slice(at, at + PART), slice(at + PART, at + 2 * PART))
        )
        out[:, h * PART : (h + 1) * PART] = (gate * jax.nn.sigmoid(gate) * up).astype(BF16)


def apply_kernel(idx, h0, h1, h2, h3, new_down, own, s1, s2, s3, full):
    x = idx[2]
    for k, h in enumerate((h0, h1, h2, h3)):
        full[block_of(x + k)] = h[...]
    width = own.shape[1]
    for k, out in enumerate((own, s1, s2, s3)):
        out[...] = nn(full[...], new_down[:, k * width : (k + 1) * width]).astype(out.dtype)


def add_kernel(idx, own, r1, r2, r3, out):
    total = own[...] + r1[...].astype(F32) + r2[...].astype(F32) + r3[...].astype(F32)
    out[...] = total.astype(out.dtype)


def join_kernel(idx, own, r1, r2, r3, came, mine, s1, s2, s3, total):
    total[...] = (
        own[...] + r1[...].astype(F32) + r2[...].astype(F32) + r3[...].astype(F32) + came[...].astype(F32)
    )
    zl = idx[4]
    for k, out in enumerate((mine, s1, s2, s3)):
        out[...] = total[block_of(zl + k)].astype(out.dtype)


def body(key_rows, value_rows, query_rows, token_rates, gate_weight, up_weight, down_weight):
    idx = jnp.stack([lax.axis_index(a) for a in ("zh", "core", "x", "y", "zl")]).astype(jnp.int32)
    tokens, width = key_rows.shape
    model = SIDE * width
    half = 3 * PART
    key_scaled = call(
        pack_kernel, "pack", [shape((tokens, 2 * width))], idx, key_rows, value_rows,
        token_rates.reshape(-1, PART), limit=2,
    )[0]

    theirs = mirrored(key_scaled)
    query_theirs = mirrored(after(query_rows, theirs))
    piece = shape((half, width))
    p = call(
        pieces_kernel, "pieces", [piece] * 5, idx, gate_weight, up_weight, down_weight,
        places=[HBM] * 3, waits=(key_scaled,), limit=4,
        scratch=[
            pltpu.VMEM((width, 8 * PART), BF16),
            pltpu.VMEM((width, 8 * PART), BF16),
            pltpu.VMEM((8 * PART, width), BF16),
            pltpu.SemaphoreType.DMA((3,)),
        ],
    )
    w = [shifted(p[SIDE - k], "y", -k) for k in range(1, SIDE)]
    stacked = call(stack_kernel, "stack", [shape((3 * half, width))], idx, *w, waits=(theirs,), limit=1)[0]
    others = swapped(stacked, "core")
    weights = call(weights_kernel, "weights", [shape((2 * half, model))], idx, p[0], *w, p[4], others)[0]

    sent_sum = shape((PART, 2 * half))
    blocks, grads = [], []
    behind, before = near_y(key_scaled)
    far = far_y(idx, behind, before)
    theirs = after(theirs, *far)
    near_theirs = near_y(theirs)

    def inner(parts, *waits, later=()):
        blocks.append(parts)
        own, *sends = call(
            sums_kernel, "sums", [shape((PART, 2 * half), F32)] + [sent_sum] * 3, idx, *parts, weights,
            waits=waits,
            scratch=[pltpu.VMEM((tokens, 2 * half), F32)], flops=2 * tokens * model * 2 * half,
        )
        pieces = scatter(own, sends, "x")
        out = call(grads_kernel, "grads", [shape((2 * half, PART))], idx, *pieces, waits=later, limit=4)[0]
        grads.append(collect_x(out))
        return pieces

    summed = inner([key_scaled, behind, *far, before])
    behind, before = near_theirs
    far = far_y(idx, behind, before, summed[0])
    arrived = inner([theirs, behind, *far, before], later=(query_theirs,))
    both = call(
        stack_kernel, "queries", [shape((2 * tokens, width))], idx, query_theirs, query_rows,
        waits=(*arrived[1:], *grads[0][1:]), limit=1,
    )[0]
    near_query = near_y(both)
    behind, before = near_query
    queries = [both, behind, *far_y(idx, behind, before, *grads[1][1:]), before]

    mine = call(
        delta_kernel, "delta", [shape((2 * half, model))], idx, *blocks[0], *blocks[1], *grads[0], *grads[1],
        waits=near_query,
        scratch=[pltpu.VMEM((2 * half, 2 * tokens), BF16)], flops=2 * 2 * tokens * model * 2 * half,
    )[0]
    partner = swapped(mine, "core")
    sent_query = shape((PART, SIDE * PART))
    *asked, new_down = call(
        query_kernel, "query", ([shape((PART, SIDE * PART), F32)] + [sent_query] * 3) * 2 + [shape((2 * PART, model))],
        idx, weights, mine, partner, *queries,
        scratch=[pltpu.VMEM((2 * half, model), BF16), pltpu.VMEM((tokens, SIDE * PART), F32)],
        flops=2 * 2 * tokens * model * SIDE * PART,
    )
    applied = []
    for c in range(2):
        own, *sends = asked[c * SIDE : (c + 1) * SIDE]
        hidden = call(silu_kernel, "silu", [shape((PART, 2 * PART))], idx, *scatter(own, sends, "x"))[0]
        own, *sends = call(
            apply_kernel, "apply", [shape((tokens, width), F32)] + [shape((tokens, width))] * 3,
            idx, *collect_x(hidden), new_down,
            scratch=[pltpu.VMEM((tokens, 2 * PART), BF16)], flops=2 * tokens * model * 2 * PART,
        )
        applied.append(scatter(own, sends, "y"))
    away = call(add_kernel, "away", [shape((tokens, width))], idx, *applied[0])[0]
    came = mirrored(away)
    own, *sends = call(
        join_kernel, "join", [shape((PART, width), F32)] + [shape((PART, width))] * 3, idx, *applied[1], came,
        scratch=[pltpu.VMEM((tokens, width), F32)],
    )
    return call(add_kernel, "last", [shape((PART, width))], idx, *scatter(own, sends, "zl"))[0]


def solution(mesh):
    fine = Mesh(mesh.devices.reshape(2, 2, SIDE, SIDE, SIDE), ("zh", "core", "x", "y", "zl"))
    dp, row, col = ("zh", "core"), ("x", "y"), "zl"
    placed = (P(dp, row), P(dp, row), P(dp, row), P(dp), P(row, col), P(row, col), P(col, row))
    return jax.shard_map(
        body, mesh=fine, in_specs=placed, out_specs=P(("zh", "core", "zl"), row), check_vma=False
    )
```

```python
import jax
import jax.numpy as jnp
from jax import lax
from jax.experimental import pallas as pl
from jax.experimental.pallas import tpu as pltpu
from jax.sharding import Mesh, PartitionSpec as P

SIDE = 4
PART = 128
BF16 = jnp.bfloat16
F32 = jnp.float32
VMEM = pl.BlockSpec(memory_space=pltpu.VMEM)
SMEM = pl.BlockSpec(memory_space=pltpu.SMEM)
ANY = pl.BlockSpec(memory_space=pl.ANY)
HBM = pl.BlockSpec(memory_space=pltpu.HBM)


def shape(dims, dtype=BF16):
    return jax.ShapeDtypeStruct(dims, dtype)


def call(kernel, name, outs, idx, *operands, waits=(), scratch=(), places=None, flops=0, limit=8):
    given = (idx, *operands, *waits)
    specs = [SMEM] + (places or [VMEM] * len(operands)) + [ANY] * len(waits)
    n_waits, n_read = len(waits), 1 + len(operands)

    def run(*refs):
        kernel(*refs[:n_read], *refs[n_read + n_waits :])

    moved = sum(o.size * o.dtype.itemsize for o in (*operands, *outs))
    return pl.pallas_call(
        run,
        out_shape=outs,
        in_specs=specs,
        out_specs=[VMEM] * len(outs),
        scratch_shapes=list(scratch),
        compiler_params=pltpu.CompilerParams(vmem_limit_bytes=limit * 2**20),
        cost_estimate=pl.CostEstimate(flops=flops, bytes_accessed=moved, transcendentals=0),
        name=name,
    )(*given)


def after(value, *others):
    return pl.pallas_call(
        lambda *refs: None,
        out_shape=shape(value.shape, value.dtype),
        in_specs=[ANY] * (1 + len(others)),
        out_specs=ANY,
        input_output_aliases={0: 0},
        compiler_params=pltpu.CompilerParams(vmem_limit_bytes=2**20),
        name="after",
    )(value, *others)


def shifted(value, axis, by):
    return lax.ppermute(value, axis, [(i, (i + by) % SIDE) for i in range(SIDE)])


def swapped(value, axis):
    return lax.ppermute(value, axis, [(0, 1), (1, 0)])


def mirrored(value):
    last = 2 * SIDE - 1
    return lax.ppermute(value, ("zh", "zl"), [(i, last - i) for i in range(2 * SIDE)])


def nt(a, b):
    return lax.dot_general(a, b, (((1,), (1,)), ((), ())), preferred_element_type=F32)


def nn(a, b):
    return jnp.dot(a, b, preferred_element_type=F32)


def block_of(at):
    return pl.ds(pl.multiple_of(lax.rem(at, SIDE) * PART, PART), PART)


def near_y(own):
    return shifted(own, "y", -1), shifted(own, "y", 1)


def far_y(idx, behind, before, *waits):
    rows, columns = before.shape
    half = shape((rows // 2, columns))
    halves = call(halves_kernel, "halves", [half, half], idx, behind, before, waits=waits, limit=1)
    return shifted(halves[0], "y", -1), shifted(halves[1], "y", 1)


def collect_x(own):
    return [own] + [shifted(own, "x", -k) for k in range(1, SIDE)]


def scatter(own, sends, axis):
    return [own] + [shifted(s, axis, k + 1) for k, s in enumerate(sends)]


def pack_kernel(idx, key, value, rates, out):
    tokens, width = key.shape
    out[:, :width] = key[...]
    for i in range(tokens // PART):
        rows = slice(i * PART, (i + 1) * PART)
        rate = jnp.broadcast_to(rates[i : i + 1], (PART, PART)).T
        for at in range(0, width, PART):
            scaled = rate * value[rows, at : at + PART].astype(F32)
            out[rows, width + at : width + at + PART] = scaled.astype(BF16)


def halves_kernel(idx, behind, before, first, second):
    half = first.shape[0]
    first[...] = behind[:half]
    second[...] = before[half:]


def stack_kernel(idx, *refs):
    *parts, out = refs
    rows = parts[0].shape[0]
    for i, part in enumerate(parts):
        out[i * rows : (i + 1) * rows] = part[...]


def pieces_kernel(idx, gate, up, down, p0, p1, p2, p3, other0, g, u, d, sems):
    window = pl.ds(pl.multiple_of(idx[0] * 8 * PART, PART), 8 * PART)
    copies = [
        pltpu.make_async_copy(gate.at[:, window], g, sems.at[0]),
        pltpu.make_async_copy(up.at[:, window], u, sems.at[1]),
        pltpu.make_async_copy(down.at[window, :], d, sems.at[2]),
    ]
    for c in copies:
        c.start()
    for c in copies:
        c.wait()
    core, y = idx[1], idx[3]
    for k, out in enumerate((p0, p1, p2, p3, other0)):
        half = core if k < SIDE else 1 - core
        at = pl.multiple_of((half * SIDE + lax.rem(y + k % SIDE, SIDE)) * PART, PART)
        out[:PART] = g[:, pl.ds(at, PART)].T
        out[PART : 2 * PART] = u[:, pl.ds(at, PART)].T
        out[2 * PART :] = d[pl.ds(at, PART), :]


def weights_kernel(idx, w0, w1, w2, w3, o0, others, full):
    rows, width = w0.shape
    for j, w in enumerate((w0, w1, w2, w3)):
        columns = slice(j * width, (j + 1) * width)
        full[:rows, columns] = w[...]
        full[rows:, columns] = o0[...] if j == 0 else others[(j - 1) * rows : j * rows]


def sums_kernel(idx, b0, b1, b2a, b2b, b3, weights, own, s1, s2, s3, total):
    size, width = b0.shape[0] // 2, b0.shape[1] // 2
    for t, far in enumerate((b2a, b2b)):
        rows = slice(t * size, (t + 1) * size)
        key, scl = (
            jnp.concatenate([b0[rows, c], b1[rows, c], far[:, c], b3[rows, c]], axis=1)
            for c in (slice(0, width), slice(width, 2 * width))
        )
        for h in range(2):
            at = h * 3 * PART
            total[rows, at : at + 2 * PART] = nt(key, weights[at : at + 2 * PART])
            total[rows, at + 2 * PART : at + 3 * PART] = nt(scl, weights[at + 2 * PART : at + 3 * PART])
    x = idx[2]
    own[...] = total[block_of(x)]
    for k, s in enumerate((s1, s2, s3)):
        s[...] = total[block_of(x + k + 1)].astype(BF16)


def grads_kernel(idx, own, r1, r2, r3, out):
    for h in range(2):
        at = h * 3 * PART
        gate, up, back = (
            own[:, c] + r1[:, c].astype(F32) + r2[:, c].astype(F32) + r3[:, c].astype(F32)
            for c in (slice(at + i * PART, at + (i + 1) * PART) for i in range(3))
        )
        s = jax.nn.sigmoid(gate)
        act = gate * s
        out[at : at + PART] = (back * up * s * (1.0 + gate * (1.0 - s))).astype(BF16).T
        out[at + PART : at + 2 * PART] = (back * act).astype(BF16).T
        out[at + 2 * PART : at + 3 * PART] = (act * up).astype(BF16).T


def delta_kernel(idx, *refs):
    blocks = [refs[0:5], refs[5:10]]
    grads = [refs[10:14], refs[14:18]]
    out, full = refs[18:]
    x = idx[2]
    tokens = SIDE * PART
    for c in range(2):
        for k in range(SIDE):
            at = pl.multiple_of(c * tokens + lax.rem(x + k, SIDE) * PART, PART)
            full[:, pl.ds(at, PART)] = grads[c][k][...]
    width = blocks[0][0].shape[1] // 2
    for j in range(SIDE):
        parts = []
        for b in blocks:
            parts += [b[2], b[3]] if j == 2 else [b[j if j < 2 else 4]]
        columns = slice(j * width, (j + 1) * width)
        key = jnp.concatenate([p[:, :width] for p in parts], axis=0)
        for h in range(2):
            at = h * 3 * PART
            out[at : at + 2 * PART, columns] = nn(full[at : at + 2 * PART], key).astype(BF16)
        scl = jnp.concatenate([p[:, width:] for p in parts], axis=0)
        for h in range(2):
            rows = slice(h * 3 * PART + 2 * PART, (h + 1) * 3 * PART)
            out[rows, columns] = nn(full[rows], scl).astype(BF16)


def ask(idx, query, fresh, outs, total):
    for h in range(2):
        rows = slice(h * 3 * PART, h * 3 * PART + 2 * PART)
        total[:, h * 2 * PART : (h + 1) * 2 * PART] = nt(query, fresh[rows])
    for k, out in enumerate(outs):
        out[...] = total[block_of(idx[2] + k)].astype(out.dtype)


def update_kernel(idx, weights, mine, theirs, q0, q1, far, q3, *refs):
    *outs, fresh, new_down, total = refs
    half, tokens = 3 * PART, SIDE * PART
    for h in range(2):
        rows, swap = slice(h * half, (h + 1) * half), slice((1 - h) * half, (2 - h) * half)
        added = mine[rows].astype(F32) + theirs[swap].astype(F32)
        fresh[rows] = (weights[rows].astype(F32) + added).astype(BF16)
        new_down[h * PART : (h + 1) * PART] = fresh[h * half + 2 * PART : (h + 1) * half]
    query = jnp.concatenate([q0[:tokens], q1[:tokens], far[...], q3[:tokens]], axis=1)
    ask(idx, query, fresh, outs, total)


def query_kernel(idx, fresh, q0, q1, far, q3, *refs):
    *outs, total = refs
    tokens = SIDE * PART
    query = jnp.concatenate([q0[tokens:], q1[tokens:], far[...], q3[tokens:]], axis=1)
    ask(idx, query, fresh, outs, total)


def silu_kernel(idx, own, r1, r2, r3, out):
    for h in range(2):
        at = h * 2 * PART
        gate, up = (
            own[:, c] + r1[:, c].astype(F32) + r2[:, c].astype(F32) + r3[:, c].astype(F32)
            for c in (slice(at, at + PART), slice(at + PART, at + 2 * PART))
        )
        out[:, h * PART : (h + 1) * PART] = (gate * jax.nn.sigmoid(gate) * up).astype(BF16)


def apply_kernel(idx, h0, h1, h2, h3, new_down, own, s1, s2, s3, full):
    x = idx[2]
    for k, h in enumerate((h0, h1, h2, h3)):
        full[block_of(x + k)] = h[...]
    width = own.shape[1]
    for k, out in enumerate((own, s1, s2, s3)):
        out[...] = nn(full[...], new_down[:, k * width : (k + 1) * width]).astype(out.dtype)


def add_kernel(idx, own, r1, r2, r3, out):
    total = own[...] + r1[...].astype(F32) + r2[...].astype(F32) + r3[...].astype(F32)
    out[...] = total.astype(out.dtype)


def join_kernel(idx, own, r1, r2, r3, came, mine, s1, s2, s3, total):
    total[...] = (
        own[...] + r1[...].astype(F32) + r2[...].astype(F32) + r3[...].astype(F32) + came[...].astype(F32)
    )
    zl = idx[4]
    for k, out in enumerate((mine, s1, s2, s3)):
        out[...] = total[block_of(zl + k)].astype(out.dtype)


def body(key_rows, value_rows, query_rows, token_rates, gate_weight, up_weight, down_weight):
    idx = jnp.stack([lax.axis_index(a) for a in ("zh", "core", "x", "y", "zl")]).astype(jnp.int32)
    tokens, width = key_rows.shape
    model = SIDE * width
    half = 3 * PART
    key_scaled = call(
        pack_kernel, "pack", [shape((tokens, 2 * width))], idx, key_rows, value_rows,
        token_rates.reshape(-1, PART), limit=2,
    )[0]

    theirs = mirrored(key_scaled)
    query_theirs = mirrored(after(query_rows, theirs))
    piece = shape((half, width))
    p = call(
        pieces_kernel, "pieces", [piece] * 5, idx, gate_weight, up_weight, down_weight,
        places=[HBM] * 3, waits=(key_scaled,), limit=4,
        scratch=[
            pltpu.VMEM((width, 8 * PART), BF16),
            pltpu.VMEM((width, 8 * PART), BF16),
            pltpu.VMEM((8 * PART, width), BF16),
            pltpu.SemaphoreType.DMA((3,)),
        ],
    )
    w = [shifted(p[SIDE - k], "y", -k) for k in range(1, SIDE)]
    stacked = call(stack_kernel, "stack", [shape((3 * half, width))], idx, *w, waits=(theirs,), limit=1)[0]
    others = swapped(stacked, "core")
    weights = call(weights_kernel, "weights", [shape((2 * half, model))], idx, p[0], *w, p[4], others)[0]

    sent_sum = shape((PART, 2 * half))
    blocks, grads = [], []
    behind, before = near_y(key_scaled)
    far = far_y(idx, behind, before)
    theirs = after(theirs, *far)
    near_theirs = near_y(theirs)

    def inner(parts, *waits, later=()):
        blocks.append(parts)
        own, *sends = call(
            sums_kernel, "sums", [shape((PART, 2 * half), F32)] + [sent_sum] * 3, idx, *parts, weights,
            waits=waits,
            scratch=[pltpu.VMEM((tokens, 2 * half), F32)], flops=2 * tokens * model * 2 * half,
        )
        pieces = scatter(own, sends, "x")
        out = call(grads_kernel, "grads", [shape((2 * half, PART))], idx, *pieces, waits=later, limit=4)[0]
        grads.append(collect_x(out))
        return pieces

    summed = inner([key_scaled, behind, *far, before])
    behind, before = near_theirs
    far = far_y(idx, behind, before, summed[0])
    arrived = inner([theirs, behind, *far, before], later=(query_theirs,))
    both = call(
        stack_kernel, "queries", [shape((2 * tokens, width))], idx, query_theirs, query_rows,
        waits=(*arrived[1:], *grads[0][1:]), limit=1,
    )[0]
    near_query = near_y(both)
    behind, before = near_query
    queries = [both, behind, *far_y(idx, behind, before, *grads[1][1:]), before]

    mine = call(
        delta_kernel, "delta", [shape((2 * half, model))], idx, *blocks[0], *blocks[1], *grads[0], *grads[1],
        waits=near_query,
        scratch=[pltpu.VMEM((2 * half, 2 * tokens), BF16)], flops=2 * 2 * tokens * model * 2 * half,
    )[0]
    partner = swapped(mine, "core")
    asks = [shape((PART, SIDE * PART), F32)] + [shape((PART, SIDE * PART))] * 3
    total = pltpu.VMEM((tokens, SIDE * PART), F32)
    q0, q1, far_first, far_second, q3 = queries
    *first, fresh, new_down = call(
        update_kernel, "update", asks + [shape((2 * half, model)), shape((2 * PART, model))],
        idx, weights, mine, partner, q0, q1, far_first, q3,
        scratch=[total], flops=2 * tokens * model * SIDE * PART,
    )
    second = call(
        query_kernel, "query", asks, idx, fresh, q0, q1, far_second, q3,
        scratch=[total], flops=2 * tokens * model * SIDE * PART,
    )
    asked = [*first, *second]
    applied = []
    for c in range(2):
        own, *sends = asked[c * SIDE : (c + 1) * SIDE]
        hidden = call(silu_kernel, "silu", [shape((PART, 2 * PART))], idx, *scatter(own, sends, "x"))[0]
        own, *sends = call(
            apply_kernel, "apply", [shape((tokens, width), F32)] + [shape((tokens, width))] * 3,
            idx, *collect_x(hidden), new_down,
            scratch=[pltpu.VMEM((tokens, 2 * PART), BF16)], flops=2 * tokens * model * 2 * PART,
        )
        applied.append(scatter(own, sends, "y"))
    away = call(add_kernel, "away", [shape((tokens, width))], idx, *applied[0])[0]
    came = mirrored(away)
    own, *sends = call(
        join_kernel, "join", [shape((PART, width), F32)] + [shape((PART, width))] * 3, idx, *applied[1], came,
        scratch=[pltpu.VMEM((tokens, width), F32)],
    )
    return call(add_kernel, "last", [shape((PART, width))], idx, *scatter(own, sends, "zl"))[0]


def solution(mesh):
    fine = Mesh(mesh.devices.reshape(2, 2, SIDE, SIDE, SIDE), ("zh", "core", "x", "y", "zl"))
    dp, row, col = ("zh", "core"), ("x", "y"), "zl"
    placed = (P(dp, row), P(dp, row), P(dp, row), P(dp), P(row, col), P(row, col), P(col, row))
    return jax.shard_map(
        body, mesh=fine, in_specs=placed, out_specs=P(("zh", "core", "zl"), row), check_vma=False
    )
```

```python
import jax
import jax.numpy as jnp
from jax import lax
from jax.experimental import pallas as pl
from jax.experimental.pallas import tpu as pltpu
from jax.sharding import Mesh, PartitionSpec as P

SIDE = 4
PART = 128
BF16 = jnp.bfloat16
F32 = jnp.float32
VMEM = pl.BlockSpec(memory_space=pltpu.VMEM)
SMEM = pl.BlockSpec(memory_space=pltpu.SMEM)
ANY = pl.BlockSpec(memory_space=pl.ANY)
HBM = pl.BlockSpec(memory_space=pltpu.HBM)


def shape(dims, dtype=BF16):
    return jax.ShapeDtypeStruct(dims, dtype)


def call(kernel, name, outs, idx, *operands, waits=(), scratch=(), places=None, flops=0, limit=8):
    given = (idx, *operands, *waits)
    specs = [SMEM] + (places or [VMEM] * len(operands)) + [ANY] * len(waits)
    n_waits, n_read = len(waits), 1 + len(operands)

    def run(*refs):
        kernel(*refs[:n_read], *refs[n_read + n_waits :])

    moved = sum(o.size * o.dtype.itemsize for o in (*operands, *outs))
    return pl.pallas_call(
        run,
        out_shape=outs,
        in_specs=specs,
        out_specs=[VMEM] * len(outs),
        scratch_shapes=list(scratch),
        compiler_params=pltpu.CompilerParams(vmem_limit_bytes=limit * 2**20),
        cost_estimate=pl.CostEstimate(flops=flops, bytes_accessed=moved, transcendentals=0),
        name=name,
    )(*given)


def after(value, *others):
    return pl.pallas_call(
        lambda *refs: None,
        out_shape=shape(value.shape, value.dtype),
        in_specs=[ANY] * (1 + len(others)),
        out_specs=ANY,
        input_output_aliases={0: 0},
        compiler_params=pltpu.CompilerParams(vmem_limit_bytes=2**20),
        name="after",
    )(value, *others)


def shifted(value, axis, by):
    return lax.ppermute(value, axis, [(i, (i + by) % SIDE) for i in range(SIDE)])


def swapped(value, axis):
    return lax.ppermute(value, axis, [(0, 1), (1, 0)])


def mirrored(value):
    last = 2 * SIDE - 1
    return lax.ppermute(value, ("zh", "zl"), [(i, last - i) for i in range(2 * SIDE)])


def nt(a, b):
    return lax.dot_general(a, b, (((1,), (1,)), ((), ())), preferred_element_type=F32)


def nn(a, b):
    return jnp.dot(a, b, preferred_element_type=F32)


def block_of(at):
    return pl.ds(pl.multiple_of(lax.rem(at, SIDE) * PART, PART), PART)


def near_y(own):
    return shifted(own, "y", -1), shifted(own, "y", 1)


def halves_y(idx, behind, before, *waits):
    rows, columns = before.shape
    half = shape((rows // 2, columns))
    return call(halves_kernel, "halves", [half, half], idx, behind, before, waits=waits, limit=1)


def far_y(halves):
    return shifted(halves[0], "y", -1), shifted(halves[1], "y", 1)


def collect_x(own):
    return [own] + [shifted(own, "x", -k) for k in range(1, SIDE)]


def scatter(own, sends, axis):
    return [own] + [shifted(s, axis, k + 1) for k, s in enumerate(sends)]


def pack_kernel(idx, key, value, rates, out):
    tokens, width = key.shape
    out[:, :width] = key[...]
    for i in range(tokens // PART):
        rows = slice(i * PART, (i + 1) * PART)
        rate = jnp.broadcast_to(rates[i : i + 1], (PART, PART)).T
        for at in range(0, width, PART):
            scaled = rate * value[rows, at : at + PART].astype(F32)
            out[rows, width + at : width + at + PART] = scaled.astype(BF16)


def halves_kernel(idx, behind, before, first, second):
    half = first.shape[0]
    first[...] = behind[:half]
    second[...] = before[half:]


def stack_kernel(idx, *refs):
    *parts, out = refs
    rows = parts[0].shape[0]
    for i, part in enumerate(parts):
        out[i * rows : (i + 1) * rows] = part[...]


def pieces_kernel(idx, gate, up, down, p0, p1, p2, p3, other0, g, u, d, sems):
    window = pl.ds(pl.multiple_of(idx[0] * 8 * PART, PART), 8 * PART)
    copies = [
        pltpu.make_async_copy(gate.at[:, window], g, sems.at[0]),
        pltpu.make_async_copy(up.at[:, window], u, sems.at[1]),
        pltpu.make_async_copy(down.at[window, :], d, sems.at[2]),
    ]
    for c in copies:
        c.start()
    for c in copies:
        c.wait()
    core, y = idx[1], idx[3]
    for k, out in enumerate((p0, p1, p2, p3, other0)):
        half = core if k < SIDE else 1 - core
        at = pl.multiple_of((half * SIDE + lax.rem(y + k % SIDE, SIDE)) * PART, PART)
        out[:PART] = g[:, pl.ds(at, PART)].T
        out[PART : 2 * PART] = u[:, pl.ds(at, PART)].T
        out[2 * PART :] = d[pl.ds(at, PART), :]


def weights_kernel(idx, w0, w1, w2, w3, o0, others, full):
    rows, width = w0.shape
    for j, w in enumerate((w0, w1, w2, w3)):
        columns = slice(j * width, (j + 1) * width)
        full[:rows, columns] = w[...]
        full[rows:, columns] = o0[...] if j == 0 else others[(j - 1) * rows : j * rows]


def sums_kernel(idx, b0, b1, b2a, b2b, b3, weights, own, s1, s2, s3, total):
    size, width = b0.shape[0] // 2, b0.shape[1] // 2
    for t, far in enumerate((b2a, b2b)):
        rows = slice(t * size, (t + 1) * size)
        key, scl = (
            jnp.concatenate([b0[rows, c], b1[rows, c], far[:, c], b3[rows, c]], axis=1)
            for c in (slice(0, width), slice(width, 2 * width))
        )
        for h in range(2):
            at = h * 3 * PART
            total[rows, at : at + 2 * PART] = nt(key, weights[at : at + 2 * PART])
            total[rows, at + 2 * PART : at + 3 * PART] = nt(scl, weights[at + 2 * PART : at + 3 * PART])
    x = idx[2]
    own[...] = total[block_of(x)]
    for k, s in enumerate((s1, s2, s3)):
        s[...] = total[block_of(x + k + 1)].astype(BF16)


def grads_kernel(idx, own, r1, r2, r3, out):
    for h in range(2):
        at = h * 3 * PART
        gate, up, back = (
            own[:, c] + r1[:, c].astype(F32) + r2[:, c].astype(F32) + r3[:, c].astype(F32)
            for c in (slice(at + i * PART, at + (i + 1) * PART) for i in range(3))
        )
        s = jax.nn.sigmoid(gate)
        act = gate * s
        out[at : at + PART] = (back * up * s * (1.0 + gate * (1.0 - s))).astype(BF16).T
        out[at + PART : at + 2 * PART] = (back * act).astype(BF16).T
        out[at + 2 * PART : at + 3 * PART] = (act * up).astype(BF16).T


def delta_kernel(idx, *refs):
    blocks = [refs[0:5], refs[5:10]]
    grads = [refs[10:14], refs[14:18]]
    out, full = refs[18:]
    x = idx[2]
    tokens = SIDE * PART
    for c in range(2):
        for k in range(SIDE):
            at = pl.multiple_of(c * tokens + lax.rem(x + k, SIDE) * PART, PART)
            full[:, pl.ds(at, PART)] = grads[c][k][...]
    width = blocks[0][0].shape[1] // 2
    for j in range(SIDE):
        parts = []
        for b in blocks:
            parts += [b[2], b[3]] if j == 2 else [b[j if j < 2 else 4]]
        columns = slice(j * width, (j + 1) * width)
        key = jnp.concatenate([p[:, :width] for p in parts], axis=0)
        for h in range(2):
            at = h * 3 * PART
            out[at : at + 2 * PART, columns] = nn(full[at : at + 2 * PART], key).astype(BF16)
        scl = jnp.concatenate([p[:, width:] for p in parts], axis=0)
        for h in range(2):
            rows = slice(h * 3 * PART + 2 * PART, (h + 1) * 3 * PART)
            out[rows, columns] = nn(full[rows], scl).astype(BF16)


def ask(idx, query, fresh, outs, total):
    for h in range(2):
        rows = slice(h * 3 * PART, h * 3 * PART + 2 * PART)
        total[:, h * 2 * PART : (h + 1) * 2 * PART] = nt(query, fresh[rows])
    for k, out in enumerate(outs):
        out[...] = total[block_of(idx[2] + k)].astype(out.dtype)


def update_kernel(idx, weights, mine, theirs, q0, q1, far, q3, *refs):
    *outs, fresh, new_down, total = refs
    half, tokens = 3 * PART, SIDE * PART
    for h in range(2):
        rows, swap = slice(h * half, (h + 1) * half), slice((1 - h) * half, (2 - h) * half)
        added = mine[rows].astype(F32) + theirs[swap].astype(F32)
        fresh[rows] = (weights[rows].astype(F32) + added).astype(BF16)
        new_down[h * PART : (h + 1) * PART] = fresh[h * half + 2 * PART : (h + 1) * half]
    query = jnp.concatenate([q0[:tokens], q1[:tokens], far[...], q3[:tokens]], axis=1)
    ask(idx, query, fresh, outs, total)


def query_kernel(idx, fresh, q0, q1, far, q3, *refs):
    *outs, total = refs
    tokens = SIDE * PART
    query = jnp.concatenate([q0[tokens:], q1[tokens:], far[...], q3[tokens:]], axis=1)
    ask(idx, query, fresh, outs, total)


def silu_kernel(idx, own, r1, r2, r3, out):
    for h in range(2):
        at = h * 2 * PART
        gate, up = (
            own[:, c] + r1[:, c].astype(F32) + r2[:, c].astype(F32) + r3[:, c].astype(F32)
            for c in (slice(at, at + PART), slice(at + PART, at + 2 * PART))
        )
        out[:, h * PART : (h + 1) * PART] = (gate * jax.nn.sigmoid(gate) * up).astype(BF16)


def apply_kernel(idx, h0, h1, h2, h3, new_down, own, s1, s2, s3, full):
    x = idx[2]
    for k, h in enumerate((h0, h1, h2, h3)):
        full[block_of(x + k)] = h[...]
    width = own.shape[1]
    for k, out in enumerate((own, s1, s2, s3)):
        out[...] = nn(full[...], new_down[:, k * width : (k + 1) * width]).astype(out.dtype)


def add_kernel(idx, own, r1, r2, r3, out):
    total = own[...] + r1[...].astype(F32) + r2[...].astype(F32) + r3[...].astype(F32)
    out[...] = total.astype(out.dtype)


def join_kernel(idx, own, r1, r2, r3, came, mine, s1, s2, s3, total):
    total[...] = (
        own[...] + r1[...].astype(F32) + r2[...].astype(F32) + r3[...].astype(F32) + came[...].astype(F32)
    )
    zl = idx[4]
    for k, out in enumerate((mine, s1, s2, s3)):
        out[...] = total[block_of(zl + k)].astype(out.dtype)


def body(key_rows, value_rows, query_rows, token_rates, gate_weight, up_weight, down_weight):
    idx = jnp.stack([lax.axis_index(a) for a in ("zh", "core", "x", "y", "zl")]).astype(jnp.int32)
    tokens, width = key_rows.shape
    model = SIDE * width
    half = 3 * PART
    key_scaled = call(
        pack_kernel, "pack", [shape((tokens, 2 * width))], idx, key_rows, value_rows,
        token_rates.reshape(-1, PART), limit=2,
    )[0]

    theirs = mirrored(key_scaled)
    query_theirs = mirrored(after(query_rows, theirs))
    piece = shape((half, width))
    p = call(
        pieces_kernel, "pieces", [piece] * 5, idx, gate_weight, up_weight, down_weight,
        places=[HBM] * 3, waits=(key_scaled,), limit=4,
        scratch=[
            pltpu.VMEM((width, 8 * PART), BF16),
            pltpu.VMEM((width, 8 * PART), BF16),
            pltpu.VMEM((8 * PART, width), BF16),
            pltpu.SemaphoreType.DMA((3,)),
        ],
    )
    w = [shifted(p[SIDE - k], "y", -k) for k in range(1, SIDE)]
    stacked = call(stack_kernel, "stack", [shape((3 * half, width))], idx, *w, waits=(theirs,), limit=1)[0]
    others = swapped(stacked, "core")
    weights = call(weights_kernel, "weights", [shape((2 * half, model))], idx, p[0], *w, p[4], others)[0]

    sent_sum = shape((PART, 2 * half))
    blocks, grads = [], []
    behind, before = near_y(key_scaled)
    far = far_y(halves_y(idx, behind, before))
    theirs = after(theirs, *far)
    near_theirs = near_y(theirs)

    def inner(parts, *waits, later=()):
        blocks.append(parts)
        own, *sends = call(
            sums_kernel, "sums", [shape((PART, 2 * half), F32)] + [sent_sum] * 3, idx, *parts, weights,
            waits=waits,
            scratch=[pltpu.VMEM((tokens, 2 * half), F32)], flops=2 * tokens * model * 2 * half,
        )
        pieces = scatter(own, sends, "x")
        out = call(grads_kernel, "grads", [shape((2 * half, PART))], idx, *pieces, waits=later, limit=4)[0]
        grads.append(collect_x(out))
        return pieces

    summed = inner([key_scaled, behind, *far, before])
    behind, before = near_theirs
    far = far_y(halves_y(idx, behind, before, summed[0]))
    arrived = inner([theirs, behind, *far, before], later=(query_theirs,))
    both = call(
        stack_kernel, "queries", [shape((2 * tokens, width))], idx, query_theirs, query_rows,
        waits=(*arrived[1:], *grads[0][1:]), limit=1,
    )[0]
    near_query = near_y(both)
    behind, before = near_query
    passed = halves_y(idx, behind, before, *grads[1][1:3])
    queries = [both, behind, *far_y(passed), before]

    mine = call(
        delta_kernel, "delta", [shape((2 * half, model))], idx, *blocks[0], *blocks[1], *grads[0], *grads[1],
        waits=passed,
        scratch=[pltpu.VMEM((2 * half, 2 * tokens), BF16)], flops=2 * 2 * tokens * model * 2 * half,
    )[0]
    partner = swapped(mine, "core")
    asks = [shape((PART, SIDE * PART), F32)] + [shape((PART, SIDE * PART))] * 3
    total = pltpu.VMEM((tokens, SIDE * PART), F32)
    q0, q1, far_first, far_second, q3 = queries
    *first, fresh, new_down = call(
        update_kernel, "update", asks + [shape((2 * half, model)), shape((2 * PART, model))],
        idx, weights, mine, partner, q0, q1, far_first, q3,
        scratch=[total], flops=2 * tokens * model * SIDE * PART,
    )
    second = call(
        query_kernel, "query", asks, idx, fresh, q0, q1, far_second, q3,
        scratch=[total], flops=2 * tokens * model * SIDE * PART,
    )
    asked = [*first, *second]
    applied = []
    for c in range(2):
        own, *sends = asked[c * SIDE : (c + 1) * SIDE]
        hidden = call(silu_kernel, "silu", [shape((PART, 2 * PART))], idx, *scatter(own, sends, "x"))[0]
        own, *sends = call(
            apply_kernel, "apply", [shape((tokens, width), F32)] + [shape((tokens, width))] * 3,
            idx, *collect_x(hidden), new_down,
            scratch=[pltpu.VMEM((tokens, 2 * PART), BF16)], flops=2 * tokens * model * 2 * PART,
        )
        applied.append(scatter(own, sends, "y"))
    away = call(add_kernel, "away", [shape((tokens, width))], idx, *applied[0])[0]
    came = mirrored(away)
    own, *sends = call(
        join_kernel, "join", [shape((PART, width), F32)] + [shape((PART, width))] * 3, idx, *applied[1], came,
        scratch=[pltpu.VMEM((tokens, width), F32)],
    )
    return call(add_kernel, "last", [shape((PART, width))], idx, *scatter(own, sends, "zl"))[0]


def solution(mesh):
    fine = Mesh(mesh.devices.reshape(2, 2, SIDE, SIDE, SIDE), ("zh", "core", "x", "y", "zl"))
    dp, row, col = ("zh", "core"), ("x", "y"), "zl"
    placed = (P(dp, row), P(dp, row), P(dp, row), P(dp), P(row, col), P(row, col), P(col, row))
    return jax.shard_map(
        body, mesh=fine, in_specs=placed, out_specs=P(("zh", "core", "zl"), row), check_vma=False
    )
```
